32 devices in a mesh: row: 2 (over x), col: 4 (over y, core), depth: 4 (over z).
Axes of the slice: x: 2, y: 2, z: 4, core: 2. Of those that a mesh axis runs over, the one named last changes fastest.
Arguments:
- tokens: bfloat16 [1024, 8192], P(('row', 'col'), 'depth'), may hold values from -6 to 6
- gate_weight: bfloat16 [8192, 14336], P(('depth', 'row'), 'col'), may hold values from -0.0625 to 0.0625
- up_weight: bfloat16 [8192, 14336], P(('depth', 'row'), 'col'), may hold values from -0.0625 to 0.0625
- down_weight: bfloat16 [14336, 8192], P(('col', 'row'), 'depth'), may hold values from -0.125 to 0.125
- gate_keep: int32 [64, 112], replicated, may hold values from 0 to 1, as said below
- up_keep: int32 [64, 112], replicated, may hold values from 0 to 1, as said below
- down_keep: int32 [112, 64], replicated, may hold values from 0 to 1, as said below
Outputs:
- mixed: bfloat16 [1024, 8192], P(('row', 'col'), 'depth')
The draws below stay inside these ranges and needn't reach their ends.
Inputs may be any that keep to these rules, and one draw needn't show every extreme that they name: `gate_keep`: 1 marks a kept block of the gate projection, 0 a dropped one. `up_keep`: 1 marks a kept block of the up projection, 0 a dropped one. `down_keep`: 1 marks a kept block of the down projection, 0 a dropped one.
All inputs are finite; a program needn't handle non-finite values.
Results may differ from the reference program's by a relative error of at most 0.005.
Values may be sent and summed in bfloat16 or wider, within the bound.
A program may use at most 128 MiB of HBM per device.

```python
import jax
import jax.numpy as jnp

D = 8192
FF = 14336
BLOCK = 128
TOKENS = 1024


def mask_levels(key):
    return jax.random.randint(jax.random.fold_in(key, 11), (FF // BLOCK,), 1, 8)


def draw_gate_keep(key, part):
    levels = mask_levels(key)
    dice_rolls = jax.random.randint(jax.random.fold_in(key, 21), (D // BLOCK, FF // BLOCK), 0, 8)
    return (dice_rolls < levels[None, :]).astype(jnp.int32)


def draw_up_keep(key, part):
    levels = mask_levels(key)
    dice_rolls = jax.random.randint(jax.random.fold_in(key, 22), (D // BLOCK, FF // BLOCK), 0, 8)
    return (dice_rolls < levels[None, :]).astype(jnp.int32)


def draw_down_keep(key, part):
    levels = mask_levels(key)
    dice_rolls = jax.random.randint(jax.random.fold_in(key, 23), (FF // BLOCK, D // BLOCK), 0, 8)
    return (dice_rolls < levels[:, None]).astype(jnp.int32)


def level_of(own_key, shape, shards, low, high):
    def one(position, shards_of):
        draws = jax.random.uniform(jax.random.fold_in(jax.random.fold_in(own_key, 6), position), (shards_of,), jnp.float32, low / len(shards), high / len(shards))
        return jnp.repeat(jnp.exp(draws), shape[position] // shards_of).reshape((-1,) + (1,) * (len(shape) - position - 1))

    level = one(*shards[0])
    for cut in shards[1:]:
        level = level * one(*cut)
    return level


def bell_draw(rng, shape, scale, most, split=(), dtype=jnp.bfloat16):
    result = scale * jax.random.normal(rng, shape, jnp.float32)
    if split:
        result = result * level_of(rng, shape, split, -0.22, 0.18)
    return jnp.clip(result, -most, most).astype(dtype)


def setup_inputs(seed: int = 0) -> dict:
    key_list = jax.random.split(jax.random.key(seed), 8)
    return {
        "tokens": bell_draw(key_list[0], (TOKENS, D), 1.0, 6.0, ((0, 8), (1, 4))),
        "gate_weight": bell_draw(key_list[1], (D, FF), D ** -0.5, 0.0625, ((0, 8), (1, 4))),
        "up_weight": bell_draw(key_list[2], (D, FF), D ** -0.5, 0.0625, ((0, 8), (1, 4))),
        "down_weight": bell_draw(key_list[3], (FF, D), (FF // 8) ** -0.5, 0.125, ((0, 8), (1, 4))),
        "gate_keep": draw_gate_keep(jax.random.fold_in(key_list[7], 71), 0),
        "up_keep": draw_up_keep(jax.random.fold_in(key_list[7], 71), 0),
        "down_keep": draw_down_keep(jax.random.fold_in(key_list[7], 71), 0),
    }


def expand_keep(keep):
    bits = keep.astype(jnp.bfloat16)
    return jnp.repeat(jnp.repeat(bits, BLOCK, axis=0), BLOCK, axis=1)


def reference(tokens, gate_weight, up_weight, down_weight, gate_keep, up_keep, down_keep):
    gate_masked = gate_weight * expand_keep(gate_keep)
    up_masked = up_weight * expand_keep(up_keep)
    down_masked = down_weight * expand_keep(down_keep)
    gate = jnp.dot(tokens, gate_masked, preferred_element_type=jnp.float32)
    up = jnp.dot(tokens, up_masked, preferred_element_type=jnp.float32)
    hidden = (jax.nn.silu(gate) * up).astype(jnp.bfloat16)
    mixed = jnp.dot(hidden, down_masked, preferred_element_type=jnp.float32)
    return mixed.astype(jnp.bfloat16)
```

```python
import functools

import jax
import jax.numpy as jnp
from jax import lax
from jax.experimental import pallas as pl
from jax.experimental.pallas import tpu as pltpu
from jax.sharding import PartitionSpec as P

BLOCK = 128
CHUNK = 256
AHEAD = 3
MESH = pl.DeviceIdType.MESH
BF16 = jnp.bfloat16
F32 = jnp.float32


def layer_kernel(
    Z, tok, gate, up, down, gate_keep, up_keep, down_keep, mixed,
    w_recv, w_own, w_mask, d_own, d_mask, part, stage, recv, hid,
    x_ss, x_rs, own_sem, d_sem, r_ss, r_rs, g_ss, g_rs,
):
    z, r, c = lax.axis_index("depth"), lax.axis_index("row"), lax.axis_index("col")
    K = w_recv.shape[0]
    rows = gate.shape[0]
    units = gate.shape[1] // 2
    shard = part.shape[2]
    features = down.shape[1]
    row_blocks = rows // BLOCK
    unit_block = (c * 2 + r) * (units // BLOCK)
    has_right, has_left = z < Z - 1, z > 0
    mirror = Z - 1 - z

    barrier = pltpu.get_barrier_semaphore()
    pl.semaphore_signal(barrier, inc=1, device_id={"row": 1 - r}, device_id_type=MESH)

    @pl.when(has_right)
    def _():
        pl.semaphore_signal(barrier, inc=1, device_id={"depth": z + 1}, device_id_type=MESH)

    @pl.when(has_left)
    def _():
        pl.semaphore_signal(barrier, inc=1, device_id={"depth": z - 1}, device_id_type=MESH)

    pl.semaphore_wait(barrier, 1 + has_right.astype(jnp.int32) + has_left.astype(jnp.int32))

    def swap(t, m):
        start = pl.multiple_of((1 - r) * units + t * CHUNK, CHUNK)
        return pltpu.make_async_remote_copy(
            src_ref=(gate, up)[m].at[:, pl.ds(start, CHUNK)],
            dst_ref=w_recv.at[t, m],
            send_sem=x_ss.at[t, m],
            recv_sem=x_rs.at[t, m],
            device_id={"row": 1 - r},
            device_id_type=MESH,
        )

    def own_copy(t, m):
        start = pl.multiple_of(r * units + t * CHUNK, CHUNK)
        slot = lax.rem(t, 2)
        return pltpu.make_async_copy(
            (gate, up)[m].at[:, pl.ds(start, CHUNK)], w_own.at[slot, m], own_sem.at[slot, m]
        )

    def down_copy(t):
        slot = lax.rem(t, 2)
        return pltpu.make_async_copy(
            down.at[pl.ds(pl.multiple_of(t * CHUNK, CHUNK), CHUNK), :], d_own.at[slot], d_sem.at[slot]
        )

    def splat(keep, i, j):
        return jnp.full((BLOCK, BLOCK), keep[i, j].astype(F32), F32).astype(BF16)

    def compute(t):
        slot = lax.rem(t, 2)

        def masked(source, src_row):
            def body(b, carry):
                at = pl.ds(pl.multiple_of(b * BLOCK, BLOCK), BLOCK)
                to = pl.ds(pl.multiple_of(src_row * rows + b * BLOCK, BLOCK), BLOCK)
                for m in range(2):
                    keep = (gate_keep, up_keep)[m]
                    for n in range(CHUNK // BLOCK):
                        s = splat(
                            keep,
                            (z * 2 + src_row) * row_blocks + b,
                            unit_block + t * (CHUNK // BLOCK) + n,
                        )
                        lo = m * CHUNK + n * BLOCK
                        w_mask[to, lo:lo + BLOCK] = (
                            source[m, at, n * BLOCK:(n + 1) * BLOCK] * s
                        )
                return carry

            lax.fori_loop(0, row_blocks, body, 0)

        for m in range(2):
            own_copy(t, m).wait()
        masked(w_own.at[slot], r)
        for m in range(2):
            swap(t, m).wait_recv()
        masked(w_recv.at[t], 1 - r)

        def rows_of(j, carry):
            block = tok[pl.ds(pl.multiple_of(j * shard, shard), shard), :]
            part[slot, j] = jnp.dot(block, w_mask[...], preferred_element_type=F32)
            return carry

        lax.fori_loop(0, Z, rows_of, 0)

    def reduce_copy(t, way, s):
        slot = lax.rem(t, 2)
        return pltpu.make_async_remote_copy(
            src_ref=stage.at[slot, way, s],
            dst_ref=recv.at[t, way, s],
            send_sem=r_ss.at[t, way, s],
            recv_sem=r_rs.at[t, way, s],
            device_id={"depth": z + 1 if way == 0 else z - 1},
            device_id_type=MESH,
        )

    ways = ((0, z, has_right), (1, mirror, has_left))

    def reduce_send(t, s):
        slot = lax.rem(t, 2)
        for way, place, open_way in ways:
            j = Z - 1 - s + place if way == 0 else s - place

            @pl.when(open_way & (place == 0))
            def _():
                stage[slot, way, s] = part[slot, j].astype(BF16)
                reduce_copy(t, way, s).start()

            if s > 0:

                @pl.when(open_way & (place > 0) & (place <= s))
                def _():
                    reduce_copy(t, way, s - 1).wait_recv()
                    stage[slot, way, s] = (
                        part[slot, j] + recv[t, way, s - 1].astype(F32)
                    ).astype(BF16)
                    reduce_copy(t, way, s).start()

    def finish(t):
        slot = lax.rem(t, 2)
        for way, place, _ in ways:

            @pl.when(place > 0)
            def _():
                reduce_copy(t, way, Z - 2).wait_recv()
                part[slot, z] = part[slot, z] + recv[t, way, Z - 2].astype(F32)

        g = part[slot, z, :, :CHUNK]
        u = part[slot, z, :, CHUNK:]
        hid[t, z] = (g / (1.0 + jnp.exp(-g)) * u).astype(BF16)

    def gather_copy(t, way, s):
        j = z - s if way == 0 else z + s
        return pltpu.make_async_remote_copy(
            src_ref=hid.at[t, j],
            dst_ref=hid.at[t, j],
            send_sem=g_ss.at[t, way, s],
            recv_sem=g_rs.at[t, way, s],
            device_id={"depth": z + 1 if way == 0 else z - 1},
            device_id_type=MESH,
        )

    def gather_send(t, s):
        for way, place, open_way in ways:

            @pl.when(open_way & (place >= s))
            def _():
                gather_copy(t, way, s).start()

    def gather_wait(t, s):
        for way, place, _ in ways:

            @pl.when(place >= s + 1)
            def _():
                j = z - 1 - s if way == 0 else z + 1 + s
                pltpu.make_async_remote_copy(
                    src_ref=hid.at[t, j],
                    dst_ref=hid.at[t, j],
                    send_sem=g_ss.at[t, way, s],
                    recv_sem=g_rs.at[t, way, s],
                    device_id={"depth": z - 1 if way == 0 else z + 1},
                    device_id_type=MESH,
                ).wait_recv()

    def add_down(t):
        slot = lax.rem(t, 2)
        down_copy(t).wait()
        wide = 512 if features % 512 == 0 else BLOCK

        def mask_cols(b, carry):
            at = pl.ds(pl.multiple_of(b * BLOCK, BLOCK), BLOCK)
            for n in range(CHUNK // BLOCK):
                s = splat(
                    down_keep,
                    unit_block + t * (CHUNK // BLOCK) + n,
                    z * (features // BLOCK) + b,
                )
                lo = n * BLOCK
                d_mask[lo:lo + BLOCK, at] = d_own[slot, lo:lo + BLOCK, at] * s
            return carry

        lax.fori_loop(0, features // BLOCK, mask_cols, 0)

        def cols_of(n, carry):
            cols = pl.ds(pl.multiple_of(n * wide, wide), wide)

            def rows_of(j, carry):
                at = pl.ds(pl.multiple_of(j * shard, shard), shard)
                mixed[at, cols] += jnp.dot(hid[t, j], d_mask[:, cols], preferred_element_type=F32)
                return carry

            return lax.fori_loop(0, Z, rows_of, carry)

        lax.fori_loop(0, features // wide, cols_of, 0)

    def settle(t):
        for m in range(2):
            swap(t, m).wait_send()
        for way, place, open_way in ways:
            for s in range(Z - 1):

                @pl.when(open_way & (place <= s))
                def _():
                    reduce_copy(t, way, s).wait_send()

                @pl.when(open_way & (place >= s))
                def _():
                    gather_copy(t, way, s).wait_send()

    for t in range(min(AHEAD, K)):
        for m in range(2):
            swap(t, m).start()
    for m in range(2):
        own_copy(0, m).start()

    def clear(j, carry):
        at = pl.ds(pl.multiple_of(j * shard, shard), shard)
        mixed[at, :] = jnp.zeros((shard, features), F32)
        return carry

    lax.fori_loop(0, Z, clear, 0)

    def slot_of(t, carry):
        @pl.when(t < K)
        def _():
            @pl.when(t + 1 < K)
            def _():
                for m in range(2):
                    own_copy(t + 1, m).start()

            down_copy(t).start()
            compute(t)

            @pl.when(t + AHEAD < K)
            def _():
                for m in range(2):
                    swap(t + AHEAD, m).start()

            reduce_send(t, 0)

        @pl.when(t > 0)
        def _():
            finish(t - 1)
            gather_send(t - 1, 0)

        for s in range(1, Z - 1):

            @pl.when(t < K)
            def _():
                reduce_send(t, s)

            @pl.when(t > 0)
            def _():
                gather_wait(t - 1, s - 1)
                gather_send(t - 1, s)

        @pl.when(t > 0)
        def _():
            gather_wait(t - 1, Z - 2)
            add_down(t - 1)
            settle(t - 1)

        return carry

    lax.fori_loop(0, K + 1, slot_of, 0)


def layer_call(tok, gate, up, down, gate_keep, up_keep, down_keep):
    Z = lax.axis_size("depth")
    T, rows = tok.shape[0], gate.shape[0]
    units, features = down.shape
    K, shard = units // CHUNK, T // Z
    dma = pltpu.SemaphoreType.DMA
    vmem = pl.BlockSpec(memory_space=pltpu.VMEM)
    smem = pl.BlockSpec(memory_space=pltpu.SMEM)
    any_space = pl.BlockSpec(memory_space=pl.ANY)
    return pl.pallas_call(
        functools.partial(layer_kernel, Z),
        out_shape=jax.ShapeDtypeStruct((T, features), F32),
        in_specs=[vmem, any_space, any_space, any_space, smem, smem, smem],
        out_specs=vmem,
        scratch_shapes=[
            pltpu.VMEM((K, 2, rows, CHUNK), BF16),
            pltpu.VMEM((2, 2, rows, CHUNK), BF16),
            pltpu.VMEM((2 * rows, 2 * CHUNK), BF16),
            pltpu.VMEM((2, CHUNK, features), BF16),
            pltpu.VMEM((CHUNK, features), BF16),
            pltpu.VMEM((2, Z, shard, 2 * CHUNK), F32),
            pltpu.VMEM((2, 2, Z - 1, shard, 2 * CHUNK), BF16),
            pltpu.VMEM((K, 2, Z - 1, shard, 2 * CHUNK), BF16),
            pltpu.VMEM((K, Z, shard, CHUNK), BF16),
            dma((K, 2)), dma((K, 2)), dma((2, 2)), dma((2,)),
            dma((K, 2, Z - 1)), dma((K, 2, Z - 1)), dma((K, 2, Z - 1)), dma((K, 2, Z - 1)),
        ],
        compiler_params=pltpu.CompilerParams(
            collective_id=0, has_side_effects=True, vmem_limit_bytes=60 * 1024 * 1024
        ),
        cost_estimate=pl.CostEstimate(
            flops=6 * T * units * features, bytes_accessed=6 * units * features, transcendentals=0
        ),
    )(tok, gate, up, down, gate_keep, up_keep, down_keep)


def keep_table(keep, row_start, col_start, row_count, col_count):
    row_ids = (row_start + jnp.arange(row_count, dtype=jnp.int32)) // BLOCK
    col_ids = (col_start + jnp.arange(col_count, dtype=jnp.int32)) // BLOCK
    pick_rows = (row_ids[:, None] == jnp.arange(keep.shape[0], dtype=jnp.int32)[None, :]).astype(BF16)
    pick_cols = (jnp.arange(keep.shape[1], dtype=jnp.int32)[:, None] == col_ids[None, :]).astype(BF16)
    inner = jnp.dot(keep.astype(BF16), pick_cols, preferred_element_type=F32).astype(BF16)
    return jnp.dot(pick_rows, inner, preferred_element_type=F32).astype(BF16)


def plain_layer(token_block, gate_weight, up_weight, down_weight, gate_keep, up_keep, down_keep):
    row_total = lax.axis_size("row")
    units, features = down_weight.shape
    feature_start = lax.axis_index("depth") * features
    unit_start = (lax.axis_index("col") * row_total + lax.axis_index("row")) * units

    def total(weight, keep):
        whole = lax.all_to_all(weight, "row", split_axis=1, concat_axis=0, tiled=True)
        masked = whole * keep_table(keep, feature_start, unit_start, features, units)
        part = jnp.dot(token_block, masked, preferred_element_type=F32)
        return lax.psum_scatter(part, "depth", scatter_dimension=0, tiled=True)

    gate = total(gate_weight, gate_keep)
    hidden = (jax.nn.silu(gate) * total(up_weight, up_keep)).astype(BF16)
    hidden = lax.all_gather(hidden, "depth", axis=0, tiled=True)
    down_masked = down_weight * keep_table(down_keep, unit_start, feature_start, units, features)
    return jnp.dot(hidden, down_masked, preferred_element_type=F32)


def on_device(tokens, gate_weight, up_weight, down_weight, *keeps):
    Z = lax.axis_size("depth")
    units, features = down_weight.shape
    token_block = lax.all_gather(tokens, ("row", "col"), axis=0, tiled=True)
    fits = (
        lax.axis_size("row") == 2
        and Z > 1
        and units % CHUNK == 0
        and gate_weight.shape[0] % BLOCK == 0
        and features % BLOCK == 0
        and token_block.shape[0] % (16 * Z) == 0
        and token_block.shape[0] <= 1024
    )
    layer = layer_call if fits else plain_layer
    mixed = layer(token_block, gate_weight, up_weight, down_weight, *keeps)
    mixed = lax.psum_scatter(mixed, ("row", "col"), scatter_dimension=0, tiled=True)
    return mixed.astype(BF16)


def solution(mesh):
    placed = (
        P(("row", "col"), "depth"),
        P(("depth", "row"), "col"),
        P(("depth", "row"), "col"),
        P(("col", "row"), "depth"),
        P(),
        P(),
        P(),
    )
    return jax.shard_map(
        on_device, mesh=mesh, in_specs=placed, out_specs=P(("row", "col"), "depth"), check_vma=False
    )
```

```python
import functools

import jax
import jax.numpy as jnp
from jax import lax
from jax.experimental import pallas as pl
from jax.experimental.pallas import tpu as pltpu
from jax.sharding import PartitionSpec as P

BLOCK = 128
CHUNK = 256
AHEAD = 3
MESH = pl.DeviceIdType.MESH
BF16 = jnp.bfloat16
F32 = jnp.float32


def layer_kernel(
    Z, tokens, gate, up, down, gate_keep, up_keep, down_keep, out,
    tok, mixed, w_recv, w_own, w_mask, d_own, d_mask, part, stage, recv, hid,
    core_recv, y_stage, y_recv, row_stage, row_recv,
    x_ss, x_rs, own_sem, d_sem, r_ss, r_rs, g_ss, g_rs, t_ss, t_rs, t_own,
    c_ss, c_rs, y_ss, y_rs, o_ss, o_rs,
):
    z, r, c = lax.axis_index("depth"), lax.axis_index("row"), lax.axis_index("col")
    K = w_recv.shape[0]
    rows = gate.shape[0]
    units = gate.shape[1] // 2
    shard = part.shape[2]
    features = down.shape[1]
    row_blocks = rows // BLOCK
    unit_block = (c * 2 + r) * (units // BLOCK)
    has_right, has_left = z < Z - 1, z > 0
    mirror = Z - 1 - z
    held = tokens.shape[0]
    wide = 512 if features % 512 == 0 else BLOCK
    pieces = features // wide
    core_mate = c + 1 - 2 * lax.rem(c, 2)
    y_mate = lax.rem(c + 2, 4)
    mates = ({"row": 1 - r}, {"col": y_mate}, {"col": core_mate})

    barrier = pltpu.get_barrier_semaphore()
    for mate in mates:
        pl.semaphore_signal(barrier, inc=1, device_id=mate, device_id_type=MESH)

    @pl.when(has_right)
    def _():
        pl.semaphore_signal(barrier, inc=1, device_id={"depth": z + 1}, device_id_type=MESH)

    @pl.when(has_left)
    def _():
        pl.semaphore_signal(barrier, inc=1, device_id={"depth": z - 1}, device_id_type=MESH)

    pl.semaphore_wait(barrier, 3 + has_right.astype(jnp.int32) + has_left.astype(jnp.int32))

    def rows_at(row, col):
        return pl.ds(pl.multiple_of((row * 4 + col) * held, held), held)

    token_moves = (
        (r, c, 1 - r, c, 0),
        (r, c, r, y_mate, 1),
        (1 - r, c, 1 - r, y_mate, 1),
        (r, c, r, core_mate, 2),
        (1 - r, c, 1 - r, core_mate, 2),
        (r, y_mate, r, lax.rem(core_mate + 2, 4), 2),
        (1 - r, y_mate, 1 - r, lax.rem(core_mate + 2, 4), 2),
    )

    def token_copy(i, arriving=False):
        row, col, back_row, back_col, mate = token_moves[i]
        at = rows_at(back_row, back_col) if arriving else rows_at(row, col)
        return pltpu.make_async_remote_copy(
            src_ref=tokens if i in (0, 1, 3) else tok.at[at],
            dst_ref=tok.at[at],
            send_sem=t_ss.at[i],
            recv_sem=t_rs.at[i],
            device_id=mates[mate],
            device_id_type=MESH,
        )

    def tokens_in():
        token_copy(0, True).wait_recv()
        token_copy(2).start()
        token_copy(4).start()
        token_copy(1, True).wait_recv()
        token_copy(5).start()
        token_copy(2, True).wait_recv()
        token_copy(6).start()
        for i in (3, 4, 5, 6):
            token_copy(i, True).wait_recv()
        for i in range(7):
            token_copy(i).wait_send()
        pltpu.make_async_copy(tokens, tok.at[rows_at(r, c)], t_own).wait()

    def swap(t, m):
        start = pl.multiple_of((1 - r) * units + t * CHUNK, CHUNK)
        return pltpu.make_async_remote_copy(
            src_ref=(gate, up)[m].at[:, pl.ds(start, CHUNK)],
            dst_ref=w_recv.at[t, m],
            send_sem=x_ss.at[t, m],
            recv_sem=x_rs.at[t, m],
            device_id={"row": 1 - r},
            device_id_type=MESH,
        )

    def own_copy(t, m):
        start = pl.multiple_of(r * units + t * CHUNK, CHUNK)
        slot = lax.rem(t, 2)
        return pltpu.make_async_copy(
            (gate, up)[m].at[:, pl.ds(start, CHUNK)], w_own.at[slot, m], own_sem.at[slot, m]
        )

    def down_copy(t):
        slot = lax.rem(t, 2)
        return pltpu.make_async_copy(
            down.at[pl.ds(pl.multiple_of(t * CHUNK, CHUNK), CHUNK), :], d_own.at[slot], d_sem.at[slot]
        )

    def splat(keep, i, j):
        return jnp.full((BLOCK, BLOCK), keep[i, j].astype(F32), F32).astype(BF16)

    def compute(t):
        slot = lax.rem(t, 2)

        def masked(source, src_row):
            def body(b, carry):
                at = pl.ds(pl.multiple_of(b * BLOCK, BLOCK), BLOCK)
                to = pl.ds(pl.multiple_of(src_row * rows + b * BLOCK, BLOCK), BLOCK)
                for m in range(2):
                    keep = (gate_keep, up_keep)[m]
                    for n in range(CHUNK // BLOCK):
                        s = splat(
                            keep,
                            (z * 2 + src_row) * row_blocks + b,
                            unit_block + t * (CHUNK // BLOCK) + n,
                        )
                        lo = m * CHUNK + n * BLOCK
                        w_mask[to, lo:lo + BLOCK] = (
                            source[m, at, n * BLOCK:(n + 1) * BLOCK] * s
                        )
                return carry

            lax.fori_loop(0, row_blocks, body, 0)

        for m in range(2):
            own_copy(t, m).wait()
        masked(w_own.at[slot], r)
        for m in range(2):
            swap(t, m).wait_recv()
        masked(w_recv.at[t], 1 - r)

        def rows_of(j, carry):
            block = tok[pl.ds(pl.multiple_of(j * shard, shard), shard), :]
            part[slot, j] = jnp.dot(block, w_mask[...], preferred_element_type=F32)
            return carry

        lax.fori_loop(0, Z, rows_of, 0)

    def reduce_copy(t, way, s):
        slot = lax.rem(t, 2)
        return pltpu.make_async_remote_copy(
            src_ref=stage.at[slot, way, s],
            dst_ref=recv.at[t, way, s],
            send_sem=r_ss.at[t, way, s],
            recv_sem=r_rs.at[t, way, s],
            device_id={"depth": z + 1 if way == 0 else z - 1},
            device_id_type=MESH,
        )

    ways = ((0, z, has_right), (1, mirror, has_left))

    def reduce_send(t, s):
        slot = lax.rem(t, 2)
        for way, place, open_way in ways:
            j = Z - 1 - s + place if way == 0 else s - place

            @pl.when(open_way & (place == 0))
            def _():
                stage[slot, way, s] = part[slot, j].astype(BF16)
                reduce_copy(t, way, s).start()

            if s > 0:

                @pl.when(open_way & (place > 0) & (place <= s))
                def _():
                    reduce_copy(t, way, s - 1).wait_recv()
                    stage[slot, way, s] = (
                        part[slot, j] + recv[t, way, s - 1].astype(F32)
                    ).astype(BF16)
                    reduce_copy(t, way, s).start()

    def finish(t):
        slot = lax.rem(t, 2)
        for way, place, _ in ways:

            @pl.when(place > 0)
            def _():
                reduce_copy(t, way, Z - 2).wait_recv()
                part[slot, z] = part[slot, z] + recv[t, way, Z - 2].astype(F32)

        g = part[slot, z, :, :CHUNK]
        u = part[slot, z, :, CHUNK:]
        hid[t, z] = (g / (1.0 + jnp.exp(-g)) * u).astype(BF16)

    def gather_copy(t, way, s):
        j = z - s if way == 0 else z + s
        return pltpu.make_async_remote_copy(
            src_ref=hid.at[t, j],
            dst_ref=hid.at[t, j],
            send_sem=g_ss.at[t, way, s],
            recv_sem=g_rs.at[t, way, s],
            device_id={"depth": z + 1 if way == 0 else z - 1},
            device_id_type=MESH,
        )

    def gather_send(t, s):
        for way, place, open_way in ways:

            @pl.when(open_way & (place >= s))
            def _():
                gather_copy(t, way, s).start()

    def gather_wait(t, s):
        for way, place, _ in ways:

            @pl.when(place >= s + 1)
            def _():
                j = z - 1 - s if way == 0 else z + 1 + s
                pltpu.make_async_remote_copy(
                    src_ref=hid.at[t, j],
                    dst_ref=hid.at[t, j],
                    send_sem=g_ss.at[t, way, s],
                    recv_sem=g_rs.at[t, way, s],
                    device_id={"depth": z - 1 if way == 0 else z + 1},
                    device_id_type=MESH,
                ).wait_recv()

    def add_down(t):
        slot = lax.rem(t, 2)
        gather_wait(t, Z - 2)
        down_copy(t).wait()

        def mask_cols(b, carry):
            at = pl.ds(pl.multiple_of(b * BLOCK, BLOCK), BLOCK)
            for n in range(CHUNK // BLOCK):
                s = splat(
                    down_keep,
                    unit_block + t * (CHUNK // BLOCK) + n,
                    z * (features // BLOCK) + b,
                )
                lo = n * BLOCK
                d_mask[lo:lo + BLOCK, at] = d_own[slot, lo:lo + BLOCK, at] * s
            return carry

        lax.fori_loop(0, features // BLOCK, mask_cols, 0)

        def cols_of(n, carry):
            cols = pl.ds(pl.multiple_of(n * wide, wide), wide)

            def rows_of(j, carry):
                at = pl.ds(pl.multiple_of(j * shard, shard), shard)
                mixed[at, cols] += jnp.dot(hid[t, j], d_mask[:, cols], preferred_element_type=F32)
                return carry

            lax.fori_loop(0, Z, rows_of, 0)

            @pl.when(t == K - 1)
            def _():
                for i in range(4):
                    core_copy(n, i).start()

            return carry

        lax.fori_loop(0, pieces, cols_of, 0)

    def settle_reduce(t):
        for m in range(2):
            swap(t, m).wait_send()
        for way, place, open_way in ways:
            for s in range(Z - 1):

                @pl.when(open_way & (place <= s))
                def _():
                    reduce_copy(t, way, s).wait_send()

    def settle_gather(t):
        for way, place, open_way in ways:
            for s in range(Z - 1):

                @pl.when(open_way & (place >= s))
                def _():
                    gather_copy(t, way, s).wait_send()

    core, y = lax.rem(c, 2), c // 2

    def cols_at(n):
        return pl.ds(pl.multiple_of(n * wide, wide), wide)

    def core_copy(n, i):
        return pltpu.make_async_remote_copy(
            src_ref=mixed.at[rows_at(i // 2, (i % 2) * 2 + 1 - core), cols_at(n)],
            dst_ref=core_recv.at[n, i],
            send_sem=c_ss.at[n, i],
            recv_sem=c_rs.at[n, i],
            device_id=mates[2],
            device_id_type=MESH,
        )

    def y_copy(n):
        return pltpu.make_async_remote_copy(
            src_ref=y_stage.at[n],
            dst_ref=y_recv.at[n],
            send_sem=y_ss.at[n],
            recv_sem=y_rs.at[n],
            device_id=mates[1],
            device_id_type=MESH,
        )

    def row_copy(n):
        return pltpu.make_async_remote_copy(
            src_ref=row_stage.at[n],
            dst_ref=row_recv.at[n],
            send_sem=o_ss.at[n],
            recv_sem=o_rs.at[n],
            device_id=mates[0],
            device_id_type=MESH,
        )

    def after_core(n, carry):
        for i in range(4):
            core_copy(n, i).wait_recv()
        for row in range(2):
            y_stage[n, row] = (
                mixed[rows_at(row, (1 - y) * 2 + core), cols_at(n)] + core_recv[n, row * 2 + 1 - y]
            ).astype(BF16)
        y_copy(n).start()
        return carry

    def after_y(n, carry):
        y_copy(n).wait_recv()
        at = rows_at(1 - r, c)
        row_stage[n] = (
            mixed[at, cols_at(n)] + core_recv[n, (1 - r) * 2 + y] + y_recv[n, 1 - r].astype(F32)
        ).astype(BF16)
        row_copy(n).start()
        return carry

    def after_row(n, carry):
        row_copy(n).wait_recv()
        out[:, cols_at(n)] = (
            mixed[rows_at(r, c), cols_at(n)]
            + core_recv[n, r * 2 + y]
            + y_recv[n, r].astype(F32)
            + row_recv[n].astype(F32)
        ).astype(BF16)
        for i in range(4):
            core_copy(n, i).wait_send()
        y_copy(n).wait_send()
        row_copy(n).wait_send()
        return carry

    for i in (0, 1, 3):
        token_copy(i).start()
    pltpu.make_async_copy(tokens, tok.at[rows_at(r, c)], t_own).start()
    for t in range(min(AHEAD, K)):
        for m in range(2):
            swap(t, m).start()
    for m in range(2):
        own_copy(0, m).start()

    def clear(j, carry):
        at = pl.ds(pl.multiple_of(j * shard, shard), shard)
        mixed[at, :] = jnp.zeros((shard, features), F32)
        return carry

    lax.fori_loop(0, Z, clear, 0)

    def slot_of(t, carry):
        @pl.when(t < K)
        def _():
            @pl.when(t + 1 < K)
            def _():
                for m in range(2):
                    own_copy(t + 1, m).start()

            compute(t)

            @pl.when(t + AHEAD < K)
            def _():
                for m in range(2):
                    swap(t + AHEAD, m).start()

            reduce_send(t, 0)

        before = (t > 0) & (t <= K)

        @pl.when(before)
        def _():
            down_copy(t - 1).start()
            finish(t - 1)
            gather_send(t - 1, 0)

        @pl.when(t > 1)
        def _():
            add_down(t - 2)

        for s in range(1, Z - 1):

            @pl.when(t < K)
            def _():
                reduce_send(t, s)

            @pl.when(before)
            def _():
                gather_wait(t - 1, s - 1)
                gather_send(t - 1, s)

        @pl.when(before)
        def _():
            settle_reduce(t - 1)

        @pl.when(t > 1)
        def _():
            settle_gather(t - 2)

        return carry

    tokens_in()
    lax.fori_loop(0, K + 2, slot_of, 0)
    lax.fori_loop(0, pieces, after_core, 0)
    lax.fori_loop(0, pieces, after_y, 0)
    lax.fori_loop(0, pieces, after_row, 0)


def layer_call(tokens, gate, up, down, gate_keep, up_keep, down_keep):
    Z = lax.axis_size("depth")
    held, rows = tokens.shape[0], gate.shape[0]
    T = held * 8
    units, features = down.shape
    K, shard = units // CHUNK, T // Z
    wide = 512 if features % 512 == 0 else BLOCK
    pieces = features // wide
    dma = pltpu.SemaphoreType.DMA
    vmem = pl.BlockSpec(memory_space=pltpu.VMEM)
    smem = pl.BlockSpec(memory_space=pltpu.SMEM)
    any_space = pl.BlockSpec(memory_space=pl.ANY)
    return pl.pallas_call(
        functools.partial(layer_kernel, Z),
        out_shape=jax.ShapeDtypeStruct((held, features), BF16),
        in_specs=[vmem, any_space, any_space, any_space, smem, smem, smem],
        out_specs=vmem,
        scratch_shapes=[
            pltpu.VMEM((T, features), BF16),
            pltpu.VMEM((T, features), F32),
            pltpu.VMEM((K, 2, rows, CHUNK), BF16),
            pltpu.VMEM((2, 2, rows, CHUNK), BF16),
            pltpu.VMEM((2 * rows, 2 * CHUNK), BF16),
            pltpu.VMEM((2, CHUNK, features), BF16),
            pltpu.VMEM((CHUNK, features), BF16),
            pltpu.VMEM((2, Z, shard, 2 * CHUNK), F32),
            pltpu.VMEM((2, 2, Z - 1, shard, 2 * CHUNK), BF16),
            pltpu.VMEM((K, 2, Z - 1, shard, 2 * CHUNK), BF16),
            pltpu.VMEM((K, Z, shard, CHUNK), BF16),
            pltpu.VMEM((pieces, 4, held, wide), F32),
            pltpu.VMEM((pieces, 2, held, wide), BF16),
            pltpu.VMEM((pieces, 2, held, wide), BF16),
            pltpu.VMEM((pieces, held, wide), BF16),
            pltpu.VMEM((pieces, held, wide), BF16),
            dma((K, 2)), dma((K, 2)), dma((2, 2)), dma((2,)),
            dma((K, 2, Z - 1)), dma((K, 2, Z - 1)), dma((K, 2, Z - 1)), dma((K, 2, Z - 1)),
            dma((7,)), dma((7,)), dma,
            dma((pieces, 4)), dma((pieces, 4)), dma((pieces,)), dma((pieces,)),
            dma((pieces,)), dma((pieces,)),
        ],
        compiler_params=pltpu.CompilerParams(
            collective_id=0, has_side_effects=True, vmem_limit_bytes=62 * 1024 * 1024
        ),
        cost_estimate=pl.CostEstimate(
            flops=6 * T * units * features, bytes_accessed=6 * units * features, transcendentals=0
        ),
    )(tokens, gate, up, down, gate_keep, up_keep, down_keep)


def keep_table(keep, row_start, col_start, row_count, col_count):
    row_ids = (row_start + jnp.arange(row_count, dtype=jnp.int32)) // BLOCK
    col_ids = (col_start + jnp.arange(col_count, dtype=jnp.int32)) // BLOCK
    pick_rows = (row_ids[:, None] == jnp.arange(keep.shape[0], dtype=jnp.int32)[None, :]).astype(BF16)
    pick_cols = (jnp.arange(keep.shape[1], dtype=jnp.int32)[:, None] == col_ids[None, :]).astype(BF16)
    inner = jnp.dot(keep.astype(BF16), pick_cols, preferred_element_type=F32).astype(BF16)
    return jnp.dot(pick_rows, inner, preferred_element_type=F32).astype(BF16)


def plain_layer(token_block, gate_weight, up_weight, down_weight, gate_keep, up_keep, down_keep):
    row_total = lax.axis_size("row")
    units, features = down_weight.shape
    feature_start = lax.axis_index("depth") * features
    unit_start = (lax.axis_index("col") * row_total + lax.axis_index("row")) * units

    def total(weight, keep):
        whole = lax.all_to_all(weight, "row", split_axis=1, concat_axis=0, tiled=True)
        masked = whole * keep_table(keep, feature_start, unit_start, features, units)
        part = jnp.dot(token_block, masked, preferred_element_type=F32)
        return lax.psum_scatter(part, "depth", scatter_dimension=0, tiled=True)

    gate = total(gate_weight, gate_keep)
    hidden = (jax.nn.silu(gate) * total(up_weight, up_keep)).astype(BF16)
    hidden = lax.all_gather(hidden, "depth", axis=0, tiled=True)
    down_masked = down_weight * keep_table(down_keep, unit_start, feature_start, units, features)
    return jnp.dot(hidden, down_masked, preferred_element_type=F32)


def on_device(tokens, gate_weight, up_weight, down_weight, *keeps):
    Z = lax.axis_size("depth")
    units, features = down_weight.shape
    fits = (
        lax.axis_size("row") == 2
        and lax.axis_size("col") == 4
        and Z > 1
        and units % CHUNK == 0
        and gate_weight.shape[0] % BLOCK == 0
        and features % BLOCK == 0
        and tokens.shape[0] * 8 % (16 * Z) == 0
        and tokens.shape[0] % 16 == 0
        and tokens.shape[0] <= 128
    )
    if fits:
        return layer_call(tokens, gate_weight, up_weight, down_weight, *keeps)
    token_block = lax.all_gather(tokens, ("row", "col"), axis=0, tiled=True)
    mixed = plain_layer(token_block, gate_weight, up_weight, down_weight, *keeps)
    mixed = lax.psum_scatter(mixed, ("row", "col"), scatter_dimension=0, tiled=True)
    return mixed.astype(BF16)


def solution(mesh):
    placed = (
        P(("row", "col"), "depth"),
        P(("depth", "row"), "col"),
        P(("depth", "row"), "col"),
        P(("col", "row"), "depth"),
        P(),
        P(),
        P(),
    )
    return jax.shard_map(
        on_device, mesh=mesh, in_specs=placed, out_specs=P(("row", "col"), "depth"), check_vma=False
    )
```

```python
import functools

import jax
import jax.numpy as jnp
from jax import lax
from jax.experimental import pallas as pl
from jax.experimental.pallas import tpu as pltpu
from jax.sharding import PartitionSpec as P

BLOCK = 128
CHUNK = 128
AHEAD = 3
MESH = pl.DeviceIdType.MESH
BF16 = jnp.bfloat16
F32 = jnp.float32


def layer_kernel(
    Z, tokens, gate, up, down, gate_keep, up_keep, down_keep, out,
    tok, mixed, w_recv, w_own, w_mask, d_own, d_mask, part, stage, recv, hid,
    core_recv, y_stage, y_recv, row_stage, row_recv,
    x_ss, x_rs, own_sem, d_sem, r_ss, r_rs, g_ss, g_rs, t_ss, t_rs, t_own,
    c_ss, c_rs, y_ss, y_rs, o_ss, o_rs,
):
    z, r, c = lax.axis_index("depth"), lax.axis_index("row"), lax.axis_index("col")
    K = w_recv.shape[0]
    rows = gate.shape[0]
    units = gate.shape[1] // 2
    shard = part.shape[2]
    features = down.shape[1]
    row_blocks = rows // BLOCK
    unit_block = (c * 2 + r) * (units // BLOCK)
    has_right, has_left = z < Z - 1, z > 0
    mirror = Z - 1 - z
    held = tokens.shape[0]
    wide = 512 if features % 512 == 0 else BLOCK
    pieces = features // wide
    core_mate = c + 1 - 2 * lax.rem(c, 2)
    y_mate = lax.rem(c + 2, 4)
    mates = ({"row": 1 - r}, {"col": y_mate}, {"col": core_mate})

    barrier = pltpu.get_barrier_semaphore()
    for mate in mates:
        pl.semaphore_signal(barrier, inc=1, device_id=mate, device_id_type=MESH)

    @pl.when(has_right)
    def _():
        pl.semaphore_signal(barrier, inc=1, device_id={"depth": z + 1}, device_id_type=MESH)

    @pl.when(has_left)
    def _():
        pl.semaphore_signal(barrier, inc=1, device_id={"depth": z - 1}, device_id_type=MESH)

    pl.semaphore_wait(barrier, 3 + has_right.astype(jnp.int32) + has_left.astype(jnp.int32))

    def rows_at(row, col):
        return pl.ds(pl.multiple_of((row * 4 + col) * held, held), held)

    token_moves = (
        (r, c, 1 - r, c, 0),
        (r, c, r, y_mate, 1),
        (1 - r, c, 1 - r, y_mate, 1),
        (r, c, r, core_mate, 2),
        (1 - r, c, 1 - r, core_mate, 2),
        (r, y_mate, r, lax.rem(core_mate + 2, 4), 2),
        (1 - r, y_mate, 1 - r, lax.rem(core_mate + 2, 4), 2),
    )

    def token_copy(i, arriving=False):
        row, col, back_row, back_col, mate = token_moves[i]
        at = rows_at(back_row, back_col) if arriving else rows_at(row, col)
        return pltpu.make_async_remote_copy(
            src_ref=tokens if i in (0, 1, 3) else tok.at[at],
            dst_ref=tok.at[at],
            send_sem=t_ss.at[i],
            recv_sem=t_rs.at[i],
            device_id=mates[mate],
            device_id_type=MESH,
        )

    def tokens_in():
        token_copy(0, True).wait_recv()
        token_copy(2).start()
        token_copy(4).start()
        token_copy(1, True).wait_recv()
        token_copy(5).start()
        token_copy(2, True).wait_recv()
        token_copy(6).start()
        for i in (3, 4, 5, 6):
            token_copy(i, True).wait_recv()
        for i in range(7):
            token_copy(i).wait_send()
        pltpu.make_async_copy(tokens, tok.at[rows_at(r, c)], t_own).wait()

    def swap(t, m):
        start = pl.multiple_of((1 - r) * units + t * CHUNK, CHUNK)
        return pltpu.make_async_remote_copy(
            src_ref=(gate, up)[m].at[:, pl.ds(start, CHUNK)],
            dst_ref=w_recv.at[t, m],
            send_sem=x_ss.at[t, m],
            recv_sem=x_rs.at[t, m],
            device_id={"row": 1 - r},
            device_id_type=MESH,
        )

    def own_copy(t, m):
        start = pl.multiple_of(r * units + t * CHUNK, CHUNK)
        slot = lax.rem(t, 2)
        return pltpu.make_async_copy(
            (gate, up)[m].at[:, pl.ds(start, CHUNK)], w_own.at[slot, m], own_sem.at[slot, m]
        )

    def down_copy(t):
        slot = lax.rem(t, 2)
        return pltpu.make_async_copy(
            down.at[pl.ds(pl.multiple_of(t * CHUNK, CHUNK), CHUNK), :], d_own.at[slot], d_sem.at[slot]
        )

    def splat(keep, i, j):
        return jnp.full((BLOCK, BLOCK), keep[i, j].astype(F32), F32).astype(BF16)

    def compute(t):
        slot = lax.rem(t, 2)

        def masked(source, src_row):
            def body(b, carry):
                at = pl.ds(pl.multiple_of(b * BLOCK, BLOCK), BLOCK)
                to = pl.ds(pl.multiple_of(src_row * rows + b * BLOCK, BLOCK), BLOCK)
                for m in range(2):
                    keep = (gate_keep, up_keep)[m]
                    for n in range(CHUNK // BLOCK):
                        s = splat(
                            keep,
                            (z * 2 + src_row) * row_blocks + b,
                            unit_block + t * (CHUNK // BLOCK) + n,
                        )
                        lo = m * CHUNK + n * BLOCK
                        w_mask[to, lo:lo + BLOCK] = (
                            source[m, at, n * BLOCK:(n + 1) * BLOCK] * s
                        )
                return carry

            lax.fori_loop(0, row_blocks, body, 0)

        for m in range(2):
            own_copy(t, m).wait()
        masked(w_own.at[slot], r)
        for m in range(2):
            swap(t, m).wait_recv()
        masked(w_recv.at[t], 1 - r)

        def rows_of(j, carry):
            block = tok[pl.ds(pl.multiple_of(j * shard, shard), shard), :]
            part[lax.rem(t, Z), j] = jnp.dot(block, w_mask[...], preferred_element_type=F32)
            return carry

        lax.fori_loop(0, Z, rows_of, 0)

    def reduce_copy(t, way, s):
        slot = lax.rem(t, 2)
        return pltpu.make_async_remote_copy(
            src_ref=stage.at[slot, way, s],
            dst_ref=recv.at[t, way, s],
            send_sem=r_ss.at[t, way, s],
            recv_sem=r_rs.at[t, way, s],
            device_id={"depth": z + 1 if way == 0 else z - 1},
            device_id_type=MESH,
        )

    ways = ((0, z, has_right), (1, mirror, has_left))

    def reduce_send(t, s):
        slot, live = lax.rem(t, 2), lax.rem(t, Z)
        for way, place, open_way in ways:
            j = Z - 1 - s + place if way == 0 else s - place

            @pl.when(open_way & (place == 0))
            def _():
                stage[slot, way, s] = part[live, j].astype(BF16)
                reduce_copy(t, way, s).start()

            if s > 0:

                @pl.when(open_way & (place > 0) & (place <= s))
                def _():
                    reduce_copy(t, way, s - 1).wait_recv()
                    stage[slot, way, s] = (
                        part[live, j] + recv[t, way, s - 1].astype(F32)
                    ).astype(BF16)
                    reduce_copy(t, way, s).start()

    def finish(t):
        live = lax.rem(t, Z)
        for way, place, _ in ways:

            @pl.when(place > 0)
            def _():
                reduce_copy(t, way, Z - 2).wait_recv()
                part[live, z] = part[live, z] + recv[t, way, Z - 2].astype(F32)

        g = part[live, z, :, :CHUNK]
        u = part[live, z, :, CHUNK:]
        hid[t, z] = (g / (1.0 + jnp.exp(-g)) * u).astype(BF16)

    def gather_copy(t, way, s):
        j = z - s if way == 0 else z + s
        return pltpu.make_async_remote_copy(
            src_ref=hid.at[t, j],
            dst_ref=hid.at[t, j],
            send_sem=g_ss.at[t, way, s],
            recv_sem=g_rs.at[t, way, s],
            device_id={"depth": z + 1 if way == 0 else z - 1},
            device_id_type=MESH,
        )

    def gather_send(t, s):
        for way, place, open_way in ways:

            @pl.when(open_way & (place >= s))
            def _():
                gather_copy(t, way, s).start()

    def gather_wait(t, s):
        for way, place, _ in ways:

            @pl.when(place >= s + 1)
            def _():
                j = z - 1 - s if way == 0 else z + 1 + s
                pltpu.make_async_remote_copy(
                    src_ref=hid.at[t, j],
                    dst_ref=hid.at[t, j],
                    send_sem=g_ss.at[t, way, s],
                    recv_sem=g_rs.at[t, way, s],
                    device_id={"depth": z - 1 if way == 0 else z + 1},
                    device_id_type=MESH,
                ).wait_recv()

    def add_down(t):
        slot = lax.rem(t, 2)
        gather_wait(t, Z - 2)
        down_copy(t).wait()

        def mask_cols(b, carry):
            at = pl.ds(pl.multiple_of(b * BLOCK, BLOCK), BLOCK)
            for n in range(CHUNK // BLOCK):
                s = splat(
                    down_keep,
                    unit_block + t * (CHUNK // BLOCK) + n,
                    z * (features // BLOCK) + b,
                )
                lo = n * BLOCK
                d_mask[lo:lo + BLOCK, at] = d_own[slot, lo:lo + BLOCK, at] * s
            return carry

        lax.fori_loop(0, features // BLOCK, mask_cols, 0)

        def cols_of(n, carry):
            cols = pl.ds(pl.multiple_of(n * wide, wide), wide)

            def rows_of(j, carry):
                at = pl.ds(pl.multiple_of(j * shard, shard), shard)
                mixed[at, cols] += jnp.dot(hid[t, j], d_mask[:, cols], preferred_element_type=F32)
                return carry

            lax.fori_loop(0, Z, rows_of, 0)

            @pl.when(t == K - 1)
            def _():
                for i in range(4):
                    core_copy(n, i).start()

            return carry

        lax.fori_loop(0, pieces, cols_of, 0)

    def settle_reduce(t, s):
        for way, place, open_way in ways:

            @pl.when(open_way & (place <= s))
            def _():
                reduce_copy(t, way, s).wait_send()

    def settle(t, carry):
        for m in range(2):
            swap(t, m).wait_send()
        for way, place, open_way in ways:
            for s in range(Z - 1):

                @pl.when(open_way & (place >= s))
                def _():
                    gather_copy(t, way, s).wait_send()

        return carry

    core, y = lax.rem(c, 2), c // 2

    def cols_at(n):
        return pl.ds(n * wide if isinstance(n, int) else pl.multiple_of(n * wide, wide), wide)

    def core_copy(n, i):
        return pltpu.make_async_remote_copy(
            src_ref=mixed.at[rows_at(i // 2, (i % 2) * 2 + 1 - core), cols_at(n)],
            dst_ref=core_recv.at[n, i],
            send_sem=c_ss.at[n, i],
            recv_sem=c_rs.at[n, i],
            device_id=mates[2],
            device_id_type=MESH,
        )

    def first_copy(n):
        return pltpu.make_async_remote_copy(
            src_ref=y_stage.at[n],
            dst_ref=y_recv.at[n],
            send_sem=y_ss.at[n],
            recv_sem=y_rs.at[n],
            device_id=mates[1 - n % 2],
            device_id_type=MESH,
        )

    def second_copy(n):
        return pltpu.make_async_remote_copy(
            src_ref=row_stage.at[n],
            dst_ref=row_recv.at[n],
            send_sem=o_ss.at[n],
            recv_sem=o_rs.at[n],
            device_id=mates[n % 2],
            device_id_type=MESH,
        )

    def chip_sum(n, row, place):
        return mixed[rows_at(row, place * 2 + core), cols_at(n)] + core_recv[n, row * 2 + place]

    def after_core(n):
        for i in range(4):
            core_copy(n, i).wait_recv()
        for i in range(2):
            total = chip_sum(n, i, 1 - y) if n % 2 == 0 else chip_sum(n, 1 - r, i)
            y_stage[n, i] = total.astype(BF16)
        first_copy(n).start()

    def after_first(n):
        first_copy(n).wait_recv()
        if n % 2 == 0:
            total = chip_sum(n, 1 - r, y) + y_recv[n, 1 - r].astype(F32)
        else:
            total = chip_sum(n, r, 1 - y) + y_recv[n, 1 - y].astype(F32)
        row_stage[n] = total.astype(BF16)
        second_copy(n).start()

    def after_second(n):
        second_copy(n).wait_recv()
        total = chip_sum(n, r, y) + y_recv[n, r if n % 2 == 0 else y].astype(F32)
        out[:, cols_at(n)] = (total + row_recv[n].astype(F32)).astype(BF16)
        for i in range(4):
            core_copy(n, i).wait_send()
        first_copy(n).wait_send()
        second_copy(n).wait_send()

    for i in (0, 1, 3):
        token_copy(i).start()
    pltpu.make_async_copy(tokens, tok.at[rows_at(r, c)], t_own).start()
    for t in range(min(AHEAD, K)):
        for m in range(2):
            swap(t, m).start()
    for m in range(2):
        own_copy(0, m).start()

    def clear(j, carry):
        at = pl.ds(pl.multiple_of(j * shard, shard), shard)
        mixed[at, :] = jnp.zeros((shard, features), F32)
        return carry

    lax.fori_loop(0, Z, clear, 0)

    def slot_of(t, carry):
        @pl.when(t < K)
        def _():
            @pl.when(t + 1 < K)
            def _():
                for m in range(2):
                    own_copy(t + 1, m).start()

            compute(t)

            @pl.when(t + AHEAD < K)
            def _():
                for m in range(2):
                    swap(t + AHEAD, m).start()

            reduce_send(t, 0)

        def at_chunk(lag, work):
            @pl.when((t >= lag) & (t < K + lag))
            def _():
                work(t - lag)

        last = 2 * Z - 2
        at_chunk(last - 1, lambda k: down_copy(k).start())
        for s in range(1, Z - 1):
            at_chunk(s, functools.partial(reduce_send, s=s))

        def finish_and_send(k):
            finish(k)
            gather_send(k, 0)

        at_chunk(Z - 1, finish_and_send)

        def pass_on(k, s):
            gather_wait(k, s - 1)
            gather_send(k, s)

        for s in range(1, Z - 1):
            at_chunk(Z - 1 + s, functools.partial(pass_on, s=s))
        at_chunk(last, add_down)
        for s in range(Z - 1):
            at_chunk(s + 1, functools.partial(settle_reduce, s=s))
        return carry

    tokens_in()
    lax.fori_loop(0, K + 2 * Z - 2, slot_of, 0)
    for n in range(pieces):
        after_core(n)
    for n in range(pieces):
        after_first(n)
    for n in range(pieces):
        after_second(n)
    lax.fori_loop(0, K, settle, 0)


def layer_call(tokens, gate, up, down, gate_keep, up_keep, down_keep):
    Z = lax.axis_size("depth")
    held, rows = tokens.shape[0], gate.shape[0]
    T = held * 8
    units, features = down.shape
    K, shard = units // CHUNK, T // Z
    wide = 512 if features % 512 == 0 else BLOCK
    pieces = features // wide
    dma = pltpu.SemaphoreType.DMA
    vmem = pl.BlockSpec(memory_space=pltpu.VMEM)
    smem = pl.BlockSpec(memory_space=pltpu.SMEM)
    any_space = pl.BlockSpec(memory_space=pl.ANY)
    return pl.pallas_call(
        functools.partial(layer_kernel, Z),
        out_shape=jax.ShapeDtypeStruct((held, features), BF16),
        in_specs=[vmem, any_space, any_space, any_space, smem, smem, smem],
        out_specs=vmem,
        scratch_shapes=[
            pltpu.VMEM((T, features), BF16),
            pltpu.VMEM((T, features), F32),
            pltpu.VMEM((K, 2, rows, CHUNK), BF16),
            pltpu.VMEM((2, 2, rows, CHUNK), BF16),
            pltpu.VMEM((2 * rows, 2 * CHUNK), BF16),
            pltpu.VMEM((2, CHUNK, features), BF16),
            pltpu.VMEM((CHUNK, features), BF16),
            pltpu.VMEM((Z, Z, shard, 2 * CHUNK), F32),
            pltpu.VMEM((2, 2, Z - 1, shard, 2 * CHUNK), BF16),
            pltpu.VMEM((K, 2, Z - 1, shard, 2 * CHUNK), BF16),
            pltpu.VMEM((K, Z, shard, CHUNK), BF16),
            pltpu.VMEM((pieces, 4, held, wide), F32),
            pltpu.VMEM((pieces, 2, held, wide), BF16),
            pltpu.VMEM((pieces, 2, held, wide), BF16),
            pltpu.VMEM((pieces, held, wide), BF16),
            pltpu.VMEM((pieces, held, wide), BF16),
            dma((K, 2)), dma((K, 2)), dma((2, 2)), dma((2,)),
            dma((K, 2, Z - 1)), dma((K, 2, Z - 1)), dma((K, 2, Z - 1)), dma((K, 2, Z - 1)),
            dma((7,)), dma((7,)), dma,
            dma((pieces, 4)), dma((pieces, 4)), dma((pieces,)), dma((pieces,)),
            dma((pieces,)), dma((pieces,)),
        ],
        compiler_params=pltpu.CompilerParams(
            collective_id=0, has_side_effects=True, vmem_limit_bytes=62 * 1024 * 1024
        ),
        cost_estimate=pl.CostEstimate(
            flops=6 * T * units * features, bytes_accessed=6 * units * features, transcendentals=0
        ),
    )(tokens, gate, up, down, gate_keep, up_keep, down_keep)


def keep_table(keep, row_start, col_start, row_count, col_count):
    row_ids = (row_start + jnp.arange(row_count, dtype=jnp.int32)) // BLOCK
    col_ids = (col_start + jnp.arange(col_count, dtype=jnp.int32)) // BLOCK
    pick_rows = (row_ids[:, None] == jnp.arange(keep.shape[0], dtype=jnp.int32)[None, :]).astype(BF16)
    pick_cols = (jnp.arange(keep.shape[1], dtype=jnp.int32)[:, None] == col_ids[None, :]).astype(BF16)
    inner = jnp.dot(keep.astype(BF16), pick_cols, preferred_element_type=F32).astype(BF16)
    return jnp.dot(pick_rows, inner, preferred_element_type=F32).astype(BF16)


def plain_layer(token_block, gate_weight, up_weight, down_weight, gate_keep, up_keep, down_keep):
    row_total = lax.axis_size("row")
    units, features = down_weight.shape
    feature_start = lax.axis_index("depth") * features
    unit_start = (lax.axis_index("col") * row_total + lax.axis_index("row")) * units

    def total(weight, keep):
        whole = lax.all_to_all(weight, "row", split_axis=1, concat_axis=0, tiled=True)
        masked = whole * keep_table(keep, feature_start, unit_start, features, units)
        part = jnp.dot(token_block, masked, preferred_element_type=F32)
        return lax.psum_scatter(part, "depth", scatter_dimension=0, tiled=True)

    gate = total(gate_weight, gate_keep)
    hidden = (jax.nn.silu(gate) * total(up_weight, up_keep)).astype(BF16)
    hidden = lax.all_gather(hidden, "depth", axis=0, tiled=True)
    down_masked = down_weight * keep_table(down_keep, unit_start, feature_start, units, features)
    return jnp.dot(hidden, down_masked, preferred_element_type=F32)


def on_device(tokens, gate_weight, up_weight, down_weight, *keeps):
    Z = lax.axis_size("depth")
    units, features = down_weight.shape
    fits = (
        lax.axis_size("row") == 2
        and lax.axis_size("col") == 4
        and Z > 1
        and units % CHUNK == 0
        and gate_weight.shape[0] % BLOCK == 0
        and features % BLOCK == 0
        and tokens.shape[0] * 8 % (16 * Z) == 0
        and tokens.shape[0] % 16 == 0
        and tokens.shape[0] <= 128
    )
    if fits:
        return layer_call(tokens, gate_weight, up_weight, down_weight, *keeps)
    token_block = lax.all_gather(tokens, ("row", "col"), axis=0, tiled=True)
    mixed = plain_layer(token_block, gate_weight, up_weight, down_weight, *keeps)
    mixed = lax.psum_scatter(mixed, ("row", "col"), scatter_dimension=0, tiled=True)
    return mixed.astype(BF16)


def solution(mesh):
    placed = (
        P(("row", "col"), "depth"),
        P(("depth", "row"), "col"),
        P(("depth", "row"), "col"),
        P(("col", "row"), "depth"),
        P(),
        P(),
        P(),
    )
    return jax.shard_map(
        on_device, mesh=mesh, in_specs=placed, out_specs=P(("row", "col"), "depth"), check_vma=False
    )
```
